32 devices in a mesh: circ: 8 (over z, y), radax: 4 (over x, core).
Axes of the slice: x: 2, y: 2, z: 4, core: 2. Of those that a mesh axis runs over, the one named last changes fastest.
Arguments:
- objective_grad: float32 [64, 64, 6, 256], P('circ', 'radax'), may hold values from -6 to 6
- adjoint_start: float32 [64, 64, 6, 256], P('circ', 'radax'), may hold values from -6 to 6
- jac_off: bfloat16 [6, 6, 64, 64, 6, 256], P(None, None, 'circ', 'radax'), may hold values from -0.625 to 0.625
- jac_diag: bfloat16 [6, 64, 64, 6, 256], P(None, 'circ', 'radax'), may hold values from -3 to 3, as said below
- precond: bfloat16 [6, 64, 64, 6, 256], P(None, 'circ', 'radax'), may hold values from -1 to 1
- face_cell: int32 [16384], P(('circ', 'radax')), may hold values from 0 to 32767
- face_side: int32 [16384], P(('circ', 'radax')), may hold values from 0 to 1
- design_grad: float32 [16384, 6, 128], P(('circ', 'radax')), may hold values from -0.0546875 to 0.0546875
Outputs:
- adjoint: float32 [64, 64, 6, 256], P('circ', 'radax')
- sensitivity: float32 [8, 128], P('circ', 'radax')
The draws below stay inside these ranges and needn't reach their ends.
Inputs may be any that keep to these rules, and one draw needn't show every extreme that they name: face_cell indexes the cells of the device that holds the face. `jac_diag`: diagonal blocks: each diagonal entry between 1.5 and 3, off-diagonal entries of moderate size.
All inputs are finite; a program needn't handle non-finite values.
Results may differ from the reference program's by a relative error of at most 0.0003.
Values sent between devices are 32-bit elements; how exact they have to be, the bound alone decides.
A program may use at most 256 MiB of HBM per device.

```python
import jax
import jax.numpy as jnp
from jax import lax

NV = 6
NDV = 128
CTH = 8
CRAD = 16
CAX = 256
FACE_DEV = 512
ITERS = 2
NTH = 64
NRAD = 64
NAX = 256
FACES = 16384
BLADES = 8
N_RADAX = 4


def dominant_blocks(key, low, high, spread):
    shape = (NV, NTH, NRAD, NV, NAX)
    first_key = jax.random.fold_in(key, 11)
    second_key = jax.random.fold_in(key, 23)
    identity = jnp.eye(NV, dtype=jnp.float32)[:, None, None, :, None]
    diagonal = jax.random.uniform(first_key, shape, jnp.float32, low, high)
    others = jnp.clip(jax.random.normal(second_key, shape, jnp.float32), -4.0, 4.0) * spread
    return identity * diagonal + (1.0 - identity) * others


def draw_jac_diag(key, part):
    return dominant_blocks(key, 1.5, 3.0, 0.4).astype(jnp.bfloat16)


def draw_precond(key, part):
    return dominant_blocks(key, 0.3, 0.6, 0.06).astype(jnp.bfloat16)


def set_ends(values, key, smallest, high):
    place = [jax.random.randint(jax.random.fold_in(key, axis), (), 0, length) for axis, length in enumerate(values.shape)]
    longest = values.shape.index(max(values.shape))
    neighbour = place[:longest] + [(place[longest] + 1) % values.shape[longest]] + place[longest + 1:]
    return values.at[tuple(place)].set(smallest).at[tuple(neighbour)].set(high)


def block_scale(key, dims, split, low, largest):
    factor_of = 1.0
    for position, blocks in split:
        draws = jax.random.uniform(jax.random.fold_in(jax.random.fold_in(key, 6), position), (blocks,), jnp.float32, low / len(split), largest / len(split))
        factor_of = factor_of * jnp.repeat(jnp.exp(draws), dims[position] // blocks).reshape((-1,) + (1,) * (len(dims) - 1 - position))
    return factor_of


def bell_draw(rng, shape, scale, reach, split=(), kind=jnp.bfloat16):
    gain = block_scale(rng, shape, split, -0.22, 0.18) if split else 1.0
    array = jax.random.normal(rng, shape, jnp.float32) * scale * gain
    return jnp.minimum(jnp.maximum(array, -reach), reach).astype(kind)


def setup_inputs(seed: int = 0) -> dict:
    splits = jax.random.split(jax.random.key(seed), 9)
    return {
        "objective_grad": bell_draw(splits[0], (NTH, NRAD, NV, NAX), 1.0, 6.0, ((0, 8), (1, 4)), jnp.float32),
        "adjoint_start": bell_draw(splits[1], (NTH, NRAD, NV, NAX), 1.0, 6.0, ((0, 8), (1, 4)), jnp.float32),
        "jac_off": bell_draw(splits[2], (6, NV, NTH, NRAD, NV, NAX), 100 ** -0.5, 0.625, ((2, 8), (3, 4))),
        "jac_diag": draw_jac_diag(jax.random.fold_in(splits[8], 71), 0),
        "precond": draw_precond(jax.random.fold_in(splits[8], 71), 0),
        "face_cell": set_ends(jax.random.randint(splits[5], (FACES,), 0, CTH * CRAD * CAX), jax.random.fold_in(splits[5], 1), 0, (CTH * CRAD * CAX) - 1).astype(jnp.int32),
        "face_side": set_ends(jax.random.randint(splits[6], (FACES,), 0, 2), jax.random.fold_in(splits[6], 1), 0, 1).astype(jnp.int32),
        "design_grad": bell_draw(splits[7], (FACES, NV, NDV), (NV * FACE_DEV * N_RADAX) ** -0.5, 0.0546875, ((0, 32),), jnp.float32),
    }


def block_apply(blocks, vector):
    summed = blocks[0].astype(jnp.float32) * vector[:, :, 0:1, :]
    for column in range(1, NV):
        summed = summed + blocks[column].astype(jnp.float32) * vector[:, :, column:column + 1, :]
    return summed


def neighbour_fields(field):
    zeros_rad = jnp.zeros_like(field[:, :1])
    zeros_ax = jnp.zeros_like(field[..., :1])
    circ_lower = jnp.roll(field, 1, axis=0)
    circ_upper = jnp.roll(field, -1, axis=0)
    rad_lower = jnp.concatenate([zeros_rad, field[:, :-1]], axis=1)
    rad_upper = jnp.concatenate([field[:, 1:], zeros_rad], axis=1)
    ax_lower = jnp.concatenate([zeros_ax, field[..., :-1]], axis=3)
    ax_upper = jnp.concatenate([field[..., 1:], zeros_ax], axis=3)
    return [circ_lower, circ_upper, rad_lower, rad_upper, ax_lower, ax_upper]


def reference(objective_grad, adjoint_start, jac_off, jac_diag, precond, face_cell, face_side, design_grad):
    adjoint = adjoint_start
    for iteration in range(ITERS):
        beside = neighbour_fields(adjoint)
        applied = block_apply(jac_diag, adjoint)
        for direction in range(6):
            applied = applied + block_apply(jac_off[direction], beside[direction])
        residual = objective_grad - applied
        adjoint = adjoint + block_apply(precond, residual)
    face_index = jnp.arange(FACES, dtype=jnp.int32)
    device = face_index // FACE_DEV
    circ_of = device // N_RADAX
    radax_of = device % N_RADAX
    local = face_cell.astype(jnp.int32)
    theta = local // (CRAD * CAX)
    radial = (local // CAX) % CRAD
    axial = local % CAX
    picked = adjoint[circ_of * CTH + theta, radax_of * CRAD + radial, :, axial]
    contrib = jnp.einsum("fi,fid->fd", picked, design_grad, precision=lax.Precision.HIGHEST)
    blade = (circ_of + face_side.astype(jnp.int32)) % BLADES
    sensitivity = jax.ops.segment_sum(contrib, blade, num_segments=BLADES)
    return adjoint, sensitivity
```

```python
import functools

import jax
import jax.numpy as jnp
from jax import lax
from jax.experimental import pallas as pl
from jax.experimental.pallas import tpu as pltpu
from jax.sharding import PartitionSpec as P

F32 = jnp.float32
BF16 = jnp.bfloat16
MESH = pl.DeviceIdType.MESH
FACE_ROWS = 128


def kernel(
    circs, rads,
    obj_hbm, adj_hbm, off_hbm, diag_hbm, pre_hbm, cell_ref, side_ref, dg_hbm,
    out_hbm, sens_ref,
    first, second, final, off, diag, pre, dg, rad_out, rad_in, picks, table, face_at, face_side,
    sens_out, sens_in,
    adj_sem, plane_sem, dg_sem, out_sem, circ_send, circ_recv, rad_send, rad_recv,
    rad2_send, rad2_recv, sens_send, sens_recv,
):
    planes, fields, rows, axial = obj_hbm.shape
    faces = cell_ref.shape[1]
    circ = lax.axis_index("circ")
    rad = lax.axis_index("radax")
    circ_up = lax.rem(circ + 1, circs)
    circ_down = lax.rem(circ + circs - 1, circs)

    def plane_loads(t):
        return [
            pltpu.make_async_copy(off_hbm.at[:, :, t], off.at[:, :, t], plane_sem.at[t, 0]),
            pltpu.make_async_copy(diag_hbm.at[:, t], diag.at[:, t], plane_sem.at[t, 1]),
            pltpu.make_async_copy(pre_hbm.at[:, t], pre.at[:, t], plane_sem.at[t, 2]),
            pltpu.make_async_copy(obj_hbm.at[t], final.at[t], plane_sem.at[t, 3]),
        ]

    adj_load = pltpu.make_async_copy(adj_hbm, first.at[pl.ds(1, planes)], adj_sem)
    dg_load = pltpu.make_async_copy(dg_hbm, dg, dg_sem)
    adj_load.start()
    order1 = [(p + planes - 3) % planes for p in range(planes)]
    for t in order1:
        for load in plane_loads(t):
            load.start()
    dg_load.start()

    barrier = pltpu.get_barrier_semaphore()
    others = [lax.rem(rad + d, rads) for d in range(1, rads)]
    for other in others:
        pl.semaphore_signal(barrier, inc=1, device_id=(circ, other), device_id_type=MESH)
    for side in (circ_up, circ_down):
        for other in [rad] + others:
            pl.semaphore_signal(barrier, inc=1, device_id=(side, other), device_id_type=MESH)
    pl.semaphore_wait(barrier, 3 * rads - 1)

    def circ_copy(application, upward):
        target = (second if application else first).at[0 if upward else planes + 1]
        if application:
            source = second.at[planes if upward else 1]
        else:
            source = adj_hbm.at[planes - 1 if upward else 0]
        return pltpu.make_async_remote_copy(
            src_ref=source, dst_ref=target,
            send_sem=circ_send.at[application, int(upward)],
            recv_sem=circ_recv.at[application, int(upward)],
            device_id=(circ_up if upward else circ_down, rad), device_id_type=MESH,
        )

    def rad_copy(upward):
        place = 0 if upward else 1
        return pltpu.make_async_remote_copy(
            src_ref=rad_out.at[0, place], dst_ref=rad_in.at[0, place],
            send_sem=rad_send.at[place], recv_sem=rad_recv.at[place],
            device_id=(circ, rad + 1 if upward else rad - 1), device_id_type=MESH,
        )

    def rad_plane_copy(upward, t):
        place = 0 if upward else 1
        return pltpu.make_async_remote_copy(
            src_ref=rad_out.at[1, place, t], dst_ref=rad_in.at[1, place, t],
            send_sem=rad2_send.at[place, t], recv_sem=rad2_recv.at[place, t],
            device_id=(circ, rad + 1 if upward else rad - 1), device_id_type=MESH,
        )

    has_lower = rad > 0
    has_upper = rad < rads - 1

    circ_copy(0, True).start()
    circ_copy(0, False).start()

    adj_load.wait()

    def edge_rows(t, carry):
        for j in range(fields):
            field = first[t + 1, j]
            rad_out[0, 0, t, j : j + 1, :] = field[rows - 1 : rows, :]
            rad_out[0, 1, t, j : j + 1, :] = field[0:1, :]
        return carry

    lax.fori_loop(0, planes, edge_rows, 0)

    @pl.when(has_upper)
    def _():
        rad_copy(True).start()

    @pl.when(has_lower)
    def _():
        rad_copy(False).start()

    @pl.when(rad == 0)
    def _():
        for application in range(2):
            rad_in[application, 0] = jnp.zeros(rad_in.shape[2:], F32)

    @pl.when(rad == rads - 1)
    def _():
        for application in range(2):
            rad_in[application, 1] = jnp.zeros(rad_in.shape[2:], F32)

    cells = cell_ref[...].astype(F32)
    row_of = jnp.floor((cells + 0.5) * (1.0 / axial))
    ax_of = cells - row_of * axial
    lanes = lax.broadcasted_iota(jnp.int32, (FACE_ROWS, planes * rows), 1).astype(F32)
    for f in range(0, faces, FACE_ROWS):
        def spread(values):
            part = values[:, f : f + FACE_ROWS]
            return jnp.transpose(jnp.broadcast_to(part, (FACE_ROWS, FACE_ROWS)))

        row_rep = spread(row_of)[:, 0:1]
        hot = jnp.where(lanes == row_rep, 1.0, 0.0).astype(BF16)
        picks[f : f + FACE_ROWS, 0 : planes * rows] = hot
        picks[f : f + FACE_ROWS, planes * rows : 2 * planes * rows] = hot
        face_at[f : f + FACE_ROWS, :] = spread(ax_of)
        face_side[f : f + FACE_ROWS, :] = spread(side_ref[...].astype(F32))

    row_index = lax.broadcasted_iota(jnp.int32, (rows, axial), 0)
    ax_index = lax.broadcasted_iota(jnp.int32, (rows, axial), 1)

    def apply_plane(source, application, t):
        def rad_lower(j):
            halo = rad_in[application, 0, t, j : j + 1, :]
            return jnp.where(row_index == 0, halo, pltpu.roll(source[t + 1, j], 1, 0))

        def rad_upper(j):
            halo = rad_in[application, 1, t, j : j + 1, :]
            return jnp.where(row_index == rows - 1, halo, pltpu.roll(source[t + 1, j], rows - 1, 0))

        def ax_lower(j):
            return jnp.where(ax_index == 0, 0.0, pltpu.roll(source[t + 1, j], 1, 1))

        def ax_upper(j):
            return jnp.where(ax_index == axial - 1, 0.0, pltpu.roll(source[t + 1, j], axial - 1, 1))

        beside = [
            lambda j: source[t, j],
            lambda j: source[t + 2, j],
            rad_lower, rad_upper, ax_lower, ax_upper,
        ]
        applied = [None] * fields
        for j in range(fields):
            vector = source[t + 1, j]
            for i in range(fields):
                term = diag[j, t, i].astype(F32) * vector
                applied[i] = term if j == 0 else applied[i] + term
        for k in range(6):
            for j in range(fields):
                vector = beside[k](j)
                for i in range(fields):
                    applied[i] = applied[i] + off[k, j, t, i].astype(F32) * vector
        residual = [final[t, i] - applied[i] for i in range(fields)]
        result = []
        for i in range(fields):
            value = pre[0, t, i].astype(F32) * residual[0]
            for j in range(1, fields):
                value = value + pre[j, t, i].astype(F32) * residual[j]
            result.append(source[t + 1, i] + value)
        return result

    @pl.when(has_lower)
    def _():
        rad_copy(True).wait_recv()

    @pl.when(has_upper)
    def _():
        rad_copy(False).wait_recv()

    def first_step(step, carry):
        t = lax.rem(step + (planes - 3), planes)

        @pl.when(step == 2)
        def _():
            circ_copy(0, True).wait_recv()
            circ_copy(0, False).wait_recv()

        for load in plane_loads(t):
            load.wait()
        result = apply_plane(first, 0, t)
        for i in range(fields):
            second[t + 1, i] = result[i]
            rad_out[1, 0, t, i : i + 1, :] = result[i][rows - 1 : rows, :]
            rad_out[1, 1, t, i : i + 1, :] = result[i][0:1, :]

        @pl.when(has_upper)
        def _():
            rad_plane_copy(True, t).start()

        @pl.when(has_lower)
        def _():
            rad_plane_copy(False, t).start()

        @pl.when(t == 0)
        def _():
            circ_copy(1, False).start()

        @pl.when(t == planes - 1)
        def _():
            circ_copy(1, True).start()

        return carry

    lax.fori_loop(0, planes, first_step, 0)

    def second_step(step, carry):
        t = lax.rem(step + 1, planes)

        @pl.when(step == planes - 2)
        def _():
            circ_copy(1, True).wait_recv()
            circ_copy(1, False).wait_recv()

        @pl.when(has_lower)
        def _():
            rad_plane_copy(True, t).wait_recv()

        @pl.when(has_upper)
        def _():
            rad_plane_copy(False, t).wait_recv()

        result = apply_plane(second, 1, t)
        for i in range(fields):
            high = result[i].astype(BF16)
            final[t, i] = result[i]
            table[i, t] = high
            table[i, t + planes] = (result[i] - high.astype(F32)).astype(BF16)
        pltpu.make_async_copy(final.at[t], out_hbm.at[t], out_sem.at[t]).start()
        return carry

    lax.fori_loop(0, planes, second_step, 0)

    dg_load.wait()
    place = lax.broadcasted_iota(jnp.int32, (FACE_ROWS, axial), 1).astype(F32)

    def face_step(step, carry):
        lower, upper = carry
        part = pl.ds(pl.multiple_of(step * FACE_ROWS, FACE_ROWS), FACE_ROWS)
        hot = picks[part, :]
        at = face_at[part, :][:, 0:1]
        side = face_side[part, :]
        total = None
        for i in range(fields):
            values = table[i].reshape(2 * planes * rows, axial)
            row = jnp.dot(hot, values, preferred_element_type=F32)
            picked = jnp.sum(jnp.where(place == at, row, 0.0), axis=1, keepdims=True)
            term = picked * dg[i, part, :]
            total = term if i == 0 else total + term
        lower = lower + jnp.sum(jnp.where(side == 0.0, total, 0.0), axis=0, keepdims=True)
        upper = upper + jnp.sum(jnp.where(side == 1.0, total, 0.0), axis=0, keepdims=True)
        return lower, upper

    zero = jnp.zeros((1, dg.shape[2]), F32)
    lower, upper = lax.fori_loop(0, faces // FACE_ROWS, face_step, (zero, zero))
    sens_out[0] = jnp.broadcast_to(lower, sens_out.shape[1:])
    sens_out[1] = jnp.broadcast_to(upper, sens_out.shape[1:])

    def sens_copy(side, d):
        return pltpu.make_async_remote_copy(
            src_ref=sens_out.at[side], dst_ref=sens_in.at[side, d],
            send_sem=sens_send.at[side, d], recv_sem=sens_recv.at[side, d],
            device_id=(circ_up if side else circ, lax.rem(rad + d, rads)), device_id_type=MESH,
        )

    sends = [(1, d) for d in range(rads)] + [(0, d) for d in range(1, rads)]
    for side, d in sends:
        sens_copy(side, d).start()
    total = lower
    for side, d in sends:
        sens_copy(side, d).wait_recv()
        total = total + sens_in[side, d, 0:1, :]
    owned = sens_ref.shape[1]
    mine = total[:, 0:owned]
    for block in range(1, rads):
        mine = jnp.where(rad == block, total[:, block * owned : (block + 1) * owned], mine)
    sens_ref[...] = mine

    for side, d in sends:
        sens_copy(side, d).wait_send()
    for application in range(2):
        for upward in (True, False):
            circ_copy(application, upward).wait_send()

    @pl.when(has_upper)
    def _():
        rad_copy(True).wait_send()
        for t in range(planes):
            rad_plane_copy(True, t).wait_send()

    @pl.when(has_lower)
    def _():
        rad_copy(False).wait_send()
        for t in range(planes):
            rad_plane_copy(False, t).wait_send()

    for t in range(planes):
        pltpu.make_async_copy(final.at[t], out_hbm.at[t], out_sem.at[t]).wait()


def body(
    objective_grad, adjoint_start, jac_off, jac_diag, precond, face_cell, face_side, design_grad
):
    circs, rads = lax.axis_size("circ"), lax.axis_size("radax")
    planes, rows, fields, axial = adjoint_start.shape
    faces, _, variables = design_grad.shape
    state = (planes, fields, rows, axial)
    any_place = pl.BlockSpec(memory_space=pl.ANY)
    in_vmem = pl.BlockSpec(memory_space=pltpu.VMEM)
    dma = pltpu.SemaphoreType.DMA
    out, sens = pl.pallas_call(
        functools.partial(kernel, circs, rads),
        out_shape=(
            jax.ShapeDtypeStruct(state, F32),
            jax.ShapeDtypeStruct((1, variables // rads), F32),
        ),
        in_specs=[any_place] * 5 + [in_vmem] * 2 + [any_place],
        out_specs=(any_place, in_vmem),
        scratch_shapes=[
            pltpu.VMEM((planes + 2, fields, rows, axial), F32),
            pltpu.VMEM((planes + 2, fields, rows, axial), F32),
            pltpu.VMEM(state, F32),
            pltpu.VMEM((6, fields) + state, BF16),
            pltpu.VMEM((fields,) + state, BF16),
            pltpu.VMEM((fields,) + state, BF16),
            pltpu.VMEM((fields, faces, variables), F32),
            pltpu.VMEM((2, 2, planes, fields, axial), F32),
            pltpu.VMEM((2, 2, planes, fields, axial), F32),
            pltpu.VMEM((faces, 2 * planes * rows), BF16),
            pltpu.VMEM((fields, 2 * planes, rows, axial), BF16),
            pltpu.VMEM((faces, FACE_ROWS), F32),
            pltpu.VMEM((faces, FACE_ROWS), F32),
            pltpu.VMEM((2, 8, variables), F32),
            pltpu.VMEM((2, rads, 8, variables), F32),
            dma, dma((planes, 4)), dma, dma((planes,)),
            dma((2, 2)), dma((2, 2)), dma((2,)), dma((2,)),
            dma((2, planes)), dma((2, planes)), dma((2, rads)), dma((2, rads)),
        ],
        compiler_params=pltpu.CompilerParams(
            collective_id=0, has_side_effects=True, vmem_limit_bytes=62 * 1024 * 1024
        ),
        cost_estimate=pl.CostEstimate(
            flops=4 * 48 * fields * planes * rows * axial,
            bytes_accessed=48 * 2 * fields * planes * rows * axial,
            transcendentals=0,
        ),
    )(
        objective_grad.transpose(0, 2, 1, 3),
        adjoint_start.transpose(0, 2, 1, 3),
        jac_off.transpose(0, 1, 2, 4, 3, 5),
        jac_diag.transpose(0, 1, 3, 2, 4),
        precond.transpose(0, 1, 3, 2, 4),
        face_cell.reshape(1, faces),
        face_side.reshape(1, faces),
        design_grad.transpose(1, 0, 2),
    )
    return out.transpose(0, 2, 1, 3), sens


def solution(mesh):
    in_specs = (
        P("circ", "radax", None, None),
        P("circ", "radax", None, None),
        P(None, None, "circ", "radax", None, None),
        P(None, "circ", "radax", None, None),
        P(None, "circ", "radax", None, None),
        P(("circ", "radax")),
        P(("circ", "radax")),
        P(("circ", "radax"), None, None),
    )
    out_specs = (P("circ", "radax", None, None), P("circ", "radax"))
    return jax.shard_map(body, mesh=mesh, in_specs=in_specs, out_specs=out_specs, check_vma=False)
```

```python
import functools

import jax
import jax.numpy as jnp
from jax import lax
from jax.experimental import pallas as pl
from jax.experimental.pallas import tpu as pltpu
from jax.sharding import PartitionSpec as P

F32 = jnp.float32
BF16 = jnp.bfloat16
MESH = pl.DeviceIdType.MESH
FACE_ROWS = 128
FACE_STEP = 256
GROUP = 3


def kernel(
    circs, rads,
    obj_hbm, adj_hbm, off_hbm, diag_hbm, pre_hbm, cell_ref, side_ref, dg_hbm,
    out_hbm, sens_ref,
    first, second, final, off, diag, pre, dg, rad_out, rad_in, picks, table, face_at, face_side, shifted, residual,
    sens_out, sens_in,
    adj_sem, plane_sem, dg_sem, out_sem, circ_send, circ_recv, rad_send, rad_recv,
    rad2_send, rad2_recv, sens_send, sens_recv,
):
    planes, fields, rows, axial = obj_hbm.shape
    faces = cell_ref.shape[1]
    circ = lax.axis_index("circ")
    rad = lax.axis_index("radax")
    circ_up = lax.rem(circ + 1, circs)
    circ_down = lax.rem(circ + circs - 1, circs)

    def plane_loads(t):
        return [
            pltpu.make_async_copy(off_hbm.at[:, :, t], off.at[:, :, t], plane_sem.at[t, 0]),
            pltpu.make_async_copy(diag_hbm.at[:, t], diag.at[:, t], plane_sem.at[t, 1]),
            pltpu.make_async_copy(pre_hbm.at[:, t], pre.at[:, t], plane_sem.at[t, 2]),
            pltpu.make_async_copy(obj_hbm.at[t], final.at[t], plane_sem.at[t, 3]),
        ]

    adj_load = pltpu.make_async_copy(adj_hbm, first.at[pl.ds(1, planes)], adj_sem)
    dg_load = pltpu.make_async_copy(dg_hbm, dg, dg_sem)
    adj_load.start()
    order1 = [(p + planes - 3) % planes for p in range(planes)]
    for t in order1:
        for load in plane_loads(t):
            load.start()
    dg_load.start()

    barrier = pltpu.get_barrier_semaphore()
    others = [lax.rem(rad + d, rads) for d in range(1, rads)]
    for other in others:
        pl.semaphore_signal(barrier, inc=1, device_id=(circ, other), device_id_type=MESH)
    for side in (circ_up, circ_down):
        for other in [rad] + others:
            pl.semaphore_signal(barrier, inc=1, device_id=(side, other), device_id_type=MESH)
    pl.semaphore_wait(barrier, 3 * rads - 1)

    def circ_copy(application, upward):
        target = (second if application else first).at[0 if upward else planes + 1]
        if application:
            source = second.at[planes if upward else 1]
        else:
            source = adj_hbm.at[planes - 1 if upward else 0]
        return pltpu.make_async_remote_copy(
            src_ref=source, dst_ref=target,
            send_sem=circ_send.at[application, int(upward)],
            recv_sem=circ_recv.at[application, int(upward)],
            device_id=(circ_up if upward else circ_down, rad), device_id_type=MESH,
        )

    def rad_copy(upward):
        place = 0 if upward else 1
        return pltpu.make_async_remote_copy(
            src_ref=rad_out.at[0, place], dst_ref=rad_in.at[0, place],
            send_sem=rad_send.at[place], recv_sem=rad_recv.at[place],
            device_id=(circ, rad + 1 if upward else rad - 1), device_id_type=MESH,
        )

    def rad_plane_copy(upward, t):
        place = 0 if upward else 1
        return pltpu.make_async_remote_copy(
            src_ref=rad_out.at[1, place, t], dst_ref=rad_in.at[1, place, t],
            send_sem=rad2_send.at[place, t], recv_sem=rad2_recv.at[place, t],
            device_id=(circ, rad + 1 if upward else rad - 1), device_id_type=MESH,
        )

    has_lower = rad > 0
    has_upper = rad < rads - 1

    circ_copy(0, True).start()
    circ_copy(0, False).start()

    adj_load.wait()

    def edge_rows(t, carry):
        for j in range(fields):
            field = first[t + 1, j]
            rad_out[0, 0, t, j : j + 1, :] = field[rows - 1 : rows, :]
            rad_out[0, 1, t, j : j + 1, :] = field[0:1, :]
        return carry

    lax.fori_loop(0, planes, edge_rows, 0)

    @pl.when(has_upper)
    def _():
        rad_copy(True).start()

    @pl.when(has_lower)
    def _():
        rad_copy(False).start()

    @pl.when(rad == 0)
    def _():
        for application in range(2):
            rad_in[application, 0] = jnp.zeros(rad_in.shape[2:], F32)

    @pl.when(rad == rads - 1)
    def _():
        for application in range(2):
            rad_in[application, 1] = jnp.zeros(rad_in.shape[2:], F32)

    cells = cell_ref[...].astype(F32)
    row_of = jnp.floor((cells + 0.5) * (1.0 / axial))
    ax_of = cells - row_of * axial
    lanes = lax.broadcasted_iota(jnp.int32, (FACE_ROWS, planes * rows), 1).astype(F32)
    for f in range(0, faces, FACE_ROWS):
        def spread(values):
            part = values[:, f : f + FACE_ROWS]
            return jnp.transpose(jnp.broadcast_to(part, (FACE_ROWS, FACE_ROWS)))

        row_rep = spread(row_of)[:, 0:1]
        hot = jnp.where(lanes == row_rep, 1.0, 0.0).astype(BF16)
        picks[f : f + FACE_ROWS, 0 : planes * rows] = hot
        picks[f : f + FACE_ROWS, planes * rows : 2 * planes * rows] = hot
        face_at[f : f + FACE_ROWS, :] = spread(ax_of)
        face_side[f : f + FACE_ROWS, :] = spread(side_ref[...].astype(F32))

    row_index = lax.broadcasted_iota(jnp.int32, (rows, axial), 0)
    ax_index = lax.broadcasted_iota(jnp.int32, (rows, axial), 1)

    def apply_plane(source, application, t, finish):
        for j in range(fields):
            centre = source[t + 1, j]
            lower = rad_in[application, 0, t, j : j + 1, :]
            upper = rad_in[application, 1, t, j : j + 1, :]
            shifted[0, j] = jnp.where(row_index == 0, lower, pltpu.roll(centre, 1, 0))
            shifted[1, j] = jnp.where(row_index == rows - 1, upper, pltpu.roll(centre, rows - 1, 0))
            shifted[2, j] = jnp.where(ax_index == 0, 0.0, pltpu.roll(centre, 1, 1))
            shifted[3, j] = jnp.where(ax_index == axial - 1, 0.0, pltpu.roll(centre, axial - 1, 1))

        def applied_group(g, carry):
            targets = [g * GROUP + i for i in range(GROUP)]
            sums = [None] * GROUP
            for j in range(fields):
                vector = source[t + 1, j]
                for n, i in enumerate(targets):
                    term = diag[j, t, i].astype(F32) * vector
                    sums[n] = term if j == 0 else sums[n] + term
            for k in range(6):
                for j in range(fields):
                    if k < 2:
                        vector = source[t + 2 * k, j]
                    else:
                        vector = shifted[k - 2, j]
                    for n, i in enumerate(targets):
                        sums[n] = sums[n] + off[k, j, t, i].astype(F32) * vector
            for n, i in enumerate(targets):
                residual[i] = final[t, i] - sums[n]
            return carry

        lax.fori_loop(0, fields // GROUP, applied_group, 0)

        def result_group(g, carry):
            targets = [g * GROUP + i for i in range(GROUP)]
            sums = [None] * GROUP
            for j in range(fields):
                vector = residual[j]
                for n, i in enumerate(targets):
                    term = pre[j, t, i].astype(F32) * vector
                    sums[n] = term if j == 0 else sums[n] + term
            for n, i in enumerate(targets):
                finish(i, source[t + 1, i] + sums[n])
            return carry

        lax.fori_loop(0, fields // GROUP, result_group, 0)

    @pl.when(has_lower)
    def _():
        rad_copy(True).wait_recv()

    @pl.when(has_upper)
    def _():
        rad_copy(False).wait_recv()

    def first_step(step, carry):
        t = lax.rem(step + (planes - 3), planes)

        @pl.when(step == 2)
        def _():
            circ_copy(0, True).wait_recv()
            circ_copy(0, False).wait_recv()

        for load in plane_loads(t):
            load.wait()

        def keep(i, value):
            second[t + 1, i] = value

        apply_plane(first, 0, t, keep)
        for i in range(fields):
            value = second[t + 1, i]
            rad_out[1, 0, t, i : i + 1, :] = value[rows - 1 : rows, :]
            rad_out[1, 1, t, i : i + 1, :] = value[0:1, :]

        @pl.when(has_upper)
        def _():
            rad_plane_copy(True, t).start()

        @pl.when(has_lower)
        def _():
            rad_plane_copy(False, t).start()

        @pl.when(t == 0)
        def _():
            circ_copy(1, False).start()

        @pl.when(t == planes - 1)
        def _():
            circ_copy(1, True).start()

        return carry

    lax.fori_loop(0, planes, first_step, 0)

    def second_step(step, carry):
        t = lax.rem(step + 1, planes)

        @pl.when(step == planes - 2)
        def _():
            circ_copy(1, True).wait_recv()
            circ_copy(1, False).wait_recv()

        @pl.when(has_lower)
        def _():
            rad_plane_copy(True, t).wait_recv()

        @pl.when(has_upper)
        def _():
            rad_plane_copy(False, t).wait_recv()

        def keep(i, value):
            high = value.astype(BF16)
            final[t, i] = value
            table[i, t] = high
            table[i, t + planes] = (value - high.astype(F32)).astype(BF16)

        apply_plane(second, 1, t, keep)
        pltpu.make_async_copy(final.at[t], out_hbm.at[t], out_sem.at[t]).start()
        return carry

    lax.fori_loop(0, planes, second_step, 0)

    dg_load.wait()
    place = lax.broadcasted_iota(jnp.int32, (FACE_STEP, axial), 1).astype(F32)
    lower = upper = jnp.zeros((1, dg.shape[2]), F32)
    for f in range(0, faces, FACE_STEP):
        part = slice(f, f + FACE_STEP)
        hot = picks[part, :]
        here = place == face_at[part, :][:, 0:1]
        side = face_side[part, :]
        total = None
        for i in range(fields):
            values = table[i].reshape(2 * planes * rows, axial)
            row = jnp.dot(hot, values, preferred_element_type=F32)
            picked = jnp.sum(jnp.where(here, row, 0.0), axis=1, keepdims=True)
            term = picked * dg[i, part, :]
            total = term if i == 0 else total + term
        lower = lower + jnp.sum(jnp.where(side == 0.0, total, 0.0), axis=0, keepdims=True)
        upper = upper + jnp.sum(jnp.where(side == 1.0, total, 0.0), axis=0, keepdims=True)
    sens_out[0] = jnp.broadcast_to(lower, sens_out.shape[1:])
    sens_out[1] = jnp.broadcast_to(upper, sens_out.shape[1:])

    def sens_copy(side, d):
        return pltpu.make_async_remote_copy(
            src_ref=sens_out.at[side], dst_ref=sens_in.at[side, d],
            send_sem=sens_send.at[side, d], recv_sem=sens_recv.at[side, d],
            device_id=(circ_up if side else circ, lax.rem(rad + d, rads)), device_id_type=MESH,
        )

    sends = [(1, d) for d in range(rads)] + [(0, d) for d in range(1, rads)]
    for side, d in sends:
        sens_copy(side, d).start()
    total = lower
    for side, d in sends:
        sens_copy(side, d).wait_recv()
        total = total + sens_in[side, d, 0:1, :]
    owned = sens_ref.shape[1]
    mine = total[:, 0:owned]
    for block in range(1, rads):
        mine = jnp.where(rad == block, total[:, block * owned : (block + 1) * owned], mine)
    sens_ref[...] = mine

    for side, d in sends:
        sens_copy(side, d).wait_send()
    for application in range(2):
        for upward in (True, False):
            circ_copy(application, upward).wait_send()

    @pl.when(has_upper)
    def _():
        rad_copy(True).wait_send()
        for t in range(planes):
            rad_plane_copy(True, t).wait_send()

    @pl.when(has_lower)
    def _():
        rad_copy(False).wait_send()
        for t in range(planes):
            rad_plane_copy(False, t).wait_send()

    for t in range(planes):
        pltpu.make_async_copy(final.at[t], out_hbm.at[t], out_sem.at[t]).wait()


def hand_over(state_ref, sens_ref, state_out, sens_out, sems):
    copies = [
        pltpu.make_async_copy(state_ref, state_out, sems.at[0]),
        pltpu.make_async_copy(sens_ref, sens_out, sems.at[1]),
    ]
    for copy in copies:
        copy.start()
    for copy in copies:
        copy.wait()


def body(
    objective_grad, adjoint_start, jac_off, jac_diag, precond, face_cell, face_side, design_grad
):
    circs, rads = lax.axis_size("circ"), lax.axis_size("radax")
    planes, rows, fields, axial = adjoint_start.shape
    faces, _, variables = design_grad.shape
    state = (planes, fields, rows, axial)
    any_place = pl.BlockSpec(memory_space=pl.ANY)
    in_vmem = pl.BlockSpec(memory_space=pltpu.VMEM)
    dma = pltpu.SemaphoreType.DMA
    out, sens = pl.pallas_call(
        functools.partial(kernel, circs, rads),
        out_shape=(
            jax.ShapeDtypeStruct(state, F32),
            jax.ShapeDtypeStruct((1, variables // rads), F32),
        ),
        in_specs=[any_place] * 5 + [in_vmem] * 2 + [any_place],
        out_specs=(any_place, in_vmem),
        scratch_shapes=[
            pltpu.VMEM((planes + 2, fields, rows, axial), F32),
            pltpu.VMEM((planes + 2, fields, rows, axial), F32),
            pltpu.VMEM(state, F32),
            pltpu.VMEM((6, fields) + state, BF16),
            pltpu.VMEM((fields,) + state, BF16),
            pltpu.VMEM((fields,) + state, BF16),
            pltpu.VMEM((fields, faces, variables), F32),
            pltpu.VMEM((2, 2, planes, fields, axial), F32),
            pltpu.VMEM((2, 2, planes, fields, axial), F32),
            pltpu.VMEM((faces, 2 * planes * rows), BF16),
            pltpu.VMEM((fields, 2 * planes, rows, axial), BF16),
            pltpu.VMEM((faces, FACE_ROWS), F32),
            pltpu.VMEM((faces, FACE_ROWS), F32),
            pltpu.VMEM((4, fields, rows, axial), F32),
            pltpu.VMEM((fields, rows, axial), F32),
            pltpu.VMEM((2, 8, variables), F32),
            pltpu.VMEM((2, rads, 8, variables), F32),
            dma, dma((planes, 4)), dma, dma((planes,)),
            dma((2, 2)), dma((2, 2)), dma((2,)), dma((2,)),
            dma((2, planes)), dma((2, planes)), dma((2, rads)), dma((2, rads)),
        ],
        compiler_params=pltpu.CompilerParams(
            collective_id=0, has_side_effects=True, vmem_limit_bytes=62 * 1024 * 1024
        ),
        cost_estimate=pl.CostEstimate(
            flops=4 * 48 * fields * planes * rows * axial,
            bytes_accessed=48 * 2 * fields * planes * rows * axial,
            transcendentals=0,
        ),
    )(
        objective_grad.transpose(0, 2, 1, 3),
        adjoint_start.transpose(0, 2, 1, 3),
        jac_off.transpose(0, 1, 2, 4, 3, 5),
        jac_diag.transpose(0, 1, 3, 2, 4),
        precond.transpose(0, 1, 3, 2, 4),
        face_cell.reshape(1, faces),
        face_side.reshape(1, faces),
        design_grad.transpose(1, 0, 2),
    )
    out, sens = pl.pallas_call(
        hand_over,
        out_shape=(
            jax.ShapeDtypeStruct(out.shape, F32),
            jax.ShapeDtypeStruct(sens.shape, F32),
        ),
        in_specs=[any_place] * 2,
        out_specs=(any_place, any_place),
        scratch_shapes=[dma((2,))],
        compiler_params=pltpu.CompilerParams(vmem_limit_bytes=62 * 1024 * 1024),
    )(out, sens)
    return out.transpose(0, 2, 1, 3), sens


def solution(mesh):
    in_specs = (
        P("circ", "radax", None, None),
        P("circ", "radax", None, None),
        P(None, None, "circ", "radax", None, None),
        P(None, "circ", "radax", None, None),
        P(None, "circ", "radax", None, None),
        P(("circ", "radax")),
        P(("circ", "radax")),
        P(("circ", "radax"), None, None),
    )
    out_specs = (P("circ", "radax", None, None), P("circ", "radax"))
    return jax.shard_map(body, mesh=mesh, in_specs=in_specs, out_specs=out_specs, check_vma=False)
```

```python
import functools

import jax
import jax.numpy as jnp
from jax import lax
from jax.experimental import pallas as pl
from jax.experimental.pallas import tpu as pltpu
from jax.sharding import PartitionSpec as P

F32 = jnp.float32
BF16 = jnp.bfloat16
MESH = pl.DeviceIdType.MESH
FACE_ROWS = 128
LAG = 4


def kernel(
    circs, rads,
    obj_hbm, adj_hbm, off_hbm, diag_hbm, pre_hbm, cell_ref, side_ref, dg_hbm,
    out_hbm, sens_ref,
    first, second, final, off, diag, pre, dg, rad_out, rad_in, picks, table, face_at, face_side,
    sens_out, sens_in,
    adj_sem, plane_sem, dg_sem, out_sem, circ_send, circ_recv, rad_send, rad_recv,
    rad2_send, rad2_recv, sens_send, sens_recv,
):
    planes, fields, rows, axial = obj_hbm.shape
    faces = cell_ref.shape[1]
    circ = lax.axis_index("circ")
    rad = lax.axis_index("radax")
    circ_up = lax.rem(circ + 1, circs)
    circ_down = lax.rem(circ + circs - 1, circs)

    def plane_loads(t):
        return [
            pltpu.make_async_copy(off_hbm.at[:, :, t], off.at[:, :, t], plane_sem.at[t, 0]),
            pltpu.make_async_copy(diag_hbm.at[:, t], diag.at[:, t], plane_sem.at[t, 1]),
            pltpu.make_async_copy(pre_hbm.at[:, t], pre.at[:, t], plane_sem.at[t, 2]),
            pltpu.make_async_copy(obj_hbm.at[t], final.at[t], plane_sem.at[t, 3]),
        ]

    adj_load = pltpu.make_async_copy(adj_hbm, first.at[pl.ds(1, planes)], adj_sem)
    dg_load = pltpu.make_async_copy(dg_hbm, dg, dg_sem)
    adj_load.start()
    order1 = [(p + 3) % planes for p in range(planes)]
    for t in order1:
        for load in plane_loads(t):
            load.start()
    dg_load.start()

    barrier = pltpu.get_barrier_semaphore()
    others = [lax.rem(rad + d, rads) for d in range(1, rads)]
    for other in others:
        pl.semaphore_signal(barrier, inc=1, device_id=(circ, other), device_id_type=MESH)
    for side in (circ_up, circ_down):
        for other in [rad] + others:
            pl.semaphore_signal(barrier, inc=1, device_id=(side, other), device_id_type=MESH)
    pl.semaphore_wait(barrier, 3 * rads - 1)

    def circ_copy(application, upward):
        target = (second if application else first).at[0 if upward else planes + 1]
        source = (second if application else first).at[planes if upward else 1]
        return pltpu.make_async_remote_copy(
            src_ref=source, dst_ref=target,
            send_sem=circ_send.at[application, int(upward)],
            recv_sem=circ_recv.at[application, int(upward)],
            device_id=(circ_up if upward else circ_down, rad), device_id_type=MESH,
        )

    def rad_copy(upward):
        place = 0 if upward else 1
        return pltpu.make_async_remote_copy(
            src_ref=rad_out.at[0, place], dst_ref=rad_in.at[0, place],
            send_sem=rad_send.at[place], recv_sem=rad_recv.at[place],
            device_id=(circ, rad + 1 if upward else rad - 1), device_id_type=MESH,
        )

    def rad_plane_copy(upward, t):
        place = 0 if upward else 1
        return pltpu.make_async_remote_copy(
            src_ref=rad_out.at[1, place, t], dst_ref=rad_in.at[1, place, t],
            send_sem=rad2_send.at[place, t], recv_sem=rad2_recv.at[place, t],
            device_id=(circ, rad + 1 if upward else rad - 1), device_id_type=MESH,
        )

    has_lower = rad > 0
    has_upper = rad < rads - 1

    adj_load.wait()
    circ_copy(0, True).start()
    circ_copy(0, False).start()

    def edge_rows(t, carry):
        for j in range(fields):
            field = first[t + 1, j]
            rad_out[0, 0, t, j : j + 1, :] = field[rows - 1 : rows, :]
            rad_out[0, 1, t, j : j + 1, :] = field[0:1, :]
        return carry

    lax.fori_loop(0, planes, edge_rows, 0)

    @pl.when(has_upper)
    def _():
        rad_copy(True).start()

    @pl.when(has_lower)
    def _():
        rad_copy(False).start()

    @pl.when(rad == 0)
    def _():
        for application in range(2):
            rad_in[application, 0] = jnp.zeros(rad_in.shape[2:], F32)

    @pl.when(rad == rads - 1)
    def _():
        for application in range(2):
            rad_in[application, 1] = jnp.zeros(rad_in.shape[2:], F32)

    cells = cell_ref[...].astype(F32)
    row_of = jnp.floor((cells + 0.5) * (1.0 / axial))
    ax_of = cells - row_of * axial
    lanes = lax.broadcasted_iota(jnp.int32, (FACE_ROWS, planes * rows), 1).astype(F32)
    for f in range(0, faces, FACE_ROWS):
        def spread(values):
            part = values[:, f : f + FACE_ROWS]
            return jnp.transpose(jnp.broadcast_to(part, (FACE_ROWS, FACE_ROWS)))

        row_rep = spread(row_of)[:, 0:1]
        hot = jnp.where(lanes == row_rep, 1.0, 0.0).astype(BF16)
        picks[f : f + FACE_ROWS, 0 : planes * rows] = hot
        picks[f : f + FACE_ROWS, planes * rows : 2 * planes * rows] = hot
        face_at[f : f + FACE_ROWS, :] = spread(ax_of)
        face_side[f : f + FACE_ROWS, :] = spread(side_ref[...].astype(F32))

    row_index = lax.broadcasted_iota(jnp.int32, (rows, axial), 0)
    ax_index = lax.broadcasted_iota(jnp.int32, (rows, axial), 1)

    def apply_plane(source, application, t):
        def rad_lower(j):
            halo = rad_in[application, 0, t, j : j + 1, :]
            return jnp.where(row_index == 0, halo, pltpu.roll(source[t + 1, j], 1, 0))

        def rad_upper(j):
            halo = rad_in[application, 1, t, j : j + 1, :]
            return jnp.where(row_index == rows - 1, halo, pltpu.roll(source[t + 1, j], rows - 1, 0))

        def ax_lower(j):
            return jnp.where(ax_index == 0, 0.0, pltpu.roll(source[t + 1, j], 1, 1))

        def ax_upper(j):
            return jnp.where(ax_index == axial - 1, 0.0, pltpu.roll(source[t + 1, j], axial - 1, 1))

        beside = [
            lambda j: source[t, j],
            lambda j: source[t + 2, j],
            rad_lower, rad_upper, ax_lower, ax_upper,
        ]
        applied = [None] * fields
        for j in range(fields):
            vector = source[t + 1, j]
            for i in range(fields):
                term = diag[j, t, i].astype(F32) * vector
                applied[i] = term if j == 0 else applied[i] + term
        for k in range(6):
            for j in range(fields):
                vector = beside[k](j)
                for i in range(fields):
                    applied[i] = applied[i] + off[k, j, t, i].astype(F32) * vector
        residual = [final[t, i] - applied[i] for i in range(fields)]
        result = []
        for i in range(fields):
            value = pre[0, t, i].astype(F32) * residual[0]
            for j in range(1, fields):
                value = value + pre[j, t, i].astype(F32) * residual[j]
            result.append(source[t + 1, i] + value)
        return result

    @pl.when(has_lower)
    def _():
        rad_copy(True).wait_recv()

    @pl.when(has_upper)
    def _():
        rad_copy(False).wait_recv()

    def circ_wait(application, t):
        @pl.when(t == 0)
        def _():
            circ_copy(application, True).wait_recv()

        @pl.when(t == planes - 1)
        def _():
            circ_copy(application, False).wait_recv()

    def first_plane(t):
        circ_wait(0, t)
        for load in plane_loads(t):
            load.wait()
        result = apply_plane(first, 0, t)
        for i in range(fields):
            second[t + 1, i] = result[i]
            rad_out[1, 0, t, i : i + 1, :] = result[i][rows - 1 : rows, :]
            rad_out[1, 1, t, i : i + 1, :] = result[i][0:1, :]

        @pl.when(has_upper)
        def _():
            rad_plane_copy(True, t).start()

        @pl.when(has_lower)
        def _():
            rad_plane_copy(False, t).start()

        @pl.when(t == 0)
        def _():
            circ_copy(1, False).start()

        @pl.when(t == planes - 1)
        def _():
            circ_copy(1, True).start()

    def second_plane(t):
        circ_wait(1, t)

        @pl.when(has_lower)
        def _():
            rad_plane_copy(True, t).wait_recv()

        @pl.when(has_upper)
        def _():
            rad_plane_copy(False, t).wait_recv()

        result = apply_plane(second, 1, t)
        for i in range(fields):
            high = result[i].astype(BF16)
            final[t, i] = result[i]
            table[i, t] = high
            table[i, t + planes] = (result[i] - high.astype(F32)).astype(BF16)
        pltpu.make_async_copy(final.at[t], out_hbm.at[t], out_sem.at[t]).start()

    def both_step(step, carry):
        @pl.when(step < planes)
        def _():
            first_plane(lax.rem(step + 3, planes))

        @pl.when(step >= LAG)
        def _():
            second_plane(lax.rem(step - LAG + 4, planes))

        return carry

    lax.fori_loop(0, planes + LAG, both_step, 0)

    dg_load.wait()
    place = lax.broadcasted_iota(jnp.int32, (FACE_ROWS, axial), 1).astype(F32)

    def face_step(step, carry):
        lower, upper = carry
        part = pl.ds(pl.multiple_of(step * FACE_ROWS, FACE_ROWS), FACE_ROWS)
        hot = picks[part, :]
        at = face_at[part, :][:, 0:1]
        side = face_side[part, :]
        total = None
        for i in range(fields):
            values = table[i].reshape(2 * planes * rows, axial)
            row = jnp.dot(hot, values, preferred_element_type=F32)
            picked = jnp.sum(jnp.where(place == at, row, 0.0), axis=1, keepdims=True)
            term = picked * dg[i, part, :]
            total = term if i == 0 else total + term
        lower = lower + jnp.sum(jnp.where(side == 0.0, total, 0.0), axis=0, keepdims=True)
        upper = upper + jnp.sum(jnp.where(side == 1.0, total, 0.0), axis=0, keepdims=True)
        return lower, upper

    zero = jnp.zeros((1, dg.shape[2]), F32)
    lower, upper = lax.fori_loop(0, faces // FACE_ROWS, face_step, (zero, zero))
    sens_out[0] = jnp.broadcast_to(lower, sens_out.shape[1:])
    sens_out[1] = jnp.broadcast_to(upper, sens_out.shape[1:])

    def sens_copy(side, d):
        return pltpu.make_async_remote_copy(
            src_ref=sens_out.at[side], dst_ref=sens_in.at[side, d],
            send_sem=sens_send.at[side, d], recv_sem=sens_recv.at[side, d],
            device_id=(circ_up if side else circ, lax.rem(rad + d, rads)), device_id_type=MESH,
        )

    sends = [(1, d) for d in range(rads)] + [(0, d) for d in range(1, rads)]
    for side, d in sends:
        sens_copy(side, d).start()
    total = lower
    for side, d in sends:
        sens_copy(side, d).wait_recv()
        total = total + sens_in[side, d, 0:1, :]
    owned = sens_ref.shape[1]
    mine = total[:, 0:owned]
    for block in range(1, rads):
        mine = jnp.where(rad == block, total[:, block * owned : (block + 1) * owned], mine)
    sens_ref[...] = mine

    for side, d in sends:
        sens_copy(side, d).wait_send()
    for application in range(2):
        for upward in (True, False):
            circ_copy(application, upward).wait_send()

    @pl.when(has_upper)
    def _():
        rad_copy(True).wait_send()
        for t in range(planes):
            rad_plane_copy(True, t).wait_send()

    @pl.when(has_lower)
    def _():
        rad_copy(False).wait_send()
        for t in range(planes):
            rad_plane_copy(False, t).wait_send()

    for t in range(planes):
        pltpu.make_async_copy(final.at[t], out_hbm.at[t], out_sem.at[t]).wait()


def hand_over(state_ref, sens_ref, state_out, sens_out, state, sens, sems):
    planes = state.shape[0]
    places = [(state_ref.at[t], state.at[t], state_out.at[t]) for t in range(planes)]
    places.append((sens_ref, sens, sens_out))
    into = [pltpu.make_async_copy(a, b, sems.at[0, n]) for n, (a, b, c) in enumerate(places)]
    onto = [pltpu.make_async_copy(b, c, sems.at[1, n]) for n, (a, b, c) in enumerate(places)]
    for copy in into:
        copy.start()
    for n, copy in enumerate(into):
        copy.wait()
        onto[n].start()
    for copy in onto:
        copy.wait()


def body(
    objective_grad, adjoint_start, jac_off, jac_diag, precond, face_cell, face_side, design_grad
):
    circs, rads = lax.axis_size("circ"), lax.axis_size("radax")
    planes, rows, fields, axial = adjoint_start.shape
    faces, _, variables = design_grad.shape
    state = (planes, fields, rows, axial)
    any_place = pl.BlockSpec(memory_space=pl.ANY)
    in_vmem = pl.BlockSpec(memory_space=pltpu.VMEM)
    dma = pltpu.SemaphoreType.DMA
    out, sens = pl.pallas_call(
        functools.partial(kernel, circs, rads),
        out_shape=(
            jax.ShapeDtypeStruct(state, F32),
            jax.ShapeDtypeStruct((1, variables // rads), F32),
        ),
        in_specs=[any_place] * 5 + [in_vmem] * 2 + [any_place],
        out_specs=(any_place, in_vmem),
        scratch_shapes=[
            pltpu.VMEM((planes + 2, fields, rows, axial), F32),
            pltpu.VMEM((planes + 2, fields, rows, axial), F32),
            pltpu.VMEM(state, F32),
            pltpu.VMEM((6, fields) + state, BF16),
            pltpu.VMEM((fields,) + state, BF16),
            pltpu.VMEM((fields,) + state, BF16),
            pltpu.VMEM((fields, faces, variables), F32),
            pltpu.VMEM((2, 2, planes, fields, axial), F32),
            pltpu.VMEM((2, 2, planes, fields, axial), F32),
            pltpu.VMEM((faces, 2 * planes * rows), BF16),
            pltpu.VMEM((fields, 2 * planes, rows, axial), BF16),
            pltpu.VMEM((faces, FACE_ROWS), F32),
            pltpu.VMEM((faces, FACE_ROWS), F32),
            pltpu.VMEM((2, 8, variables), F32),
            pltpu.VMEM((2, rads, 8, variables), F32),
            dma, dma((planes, 4)), dma, dma((planes,)),
            dma((2, 2)), dma((2, 2)), dma((2,)), dma((2,)),
            dma((2, planes)), dma((2, planes)), dma((2, rads)), dma((2, rads)),
        ],
        compiler_params=pltpu.CompilerParams(
            collective_id=0, has_side_effects=True, vmem_limit_bytes=62 * 1024 * 1024
        ),
        cost_estimate=pl.CostEstimate(
            flops=4 * 48 * fields * planes * rows * axial,
            bytes_accessed=48 * 2 * fields * planes * rows * axial,
            transcendentals=0,
        ),
    )(
        objective_grad.transpose(0, 2, 1, 3),
        adjoint_start.transpose(0, 2, 1, 3),
        jac_off.transpose(0, 1, 2, 4, 3, 5),
        jac_diag.transpose(0, 1, 3, 2, 4),
        precond.transpose(0, 1, 3, 2, 4),
        face_cell.reshape(1, faces),
        face_side.reshape(1, faces),
        design_grad.transpose(1, 0, 2),
    )
    out, sens = pl.pallas_call(
        hand_over,
        out_shape=(
            jax.ShapeDtypeStruct(out.shape, F32),
            jax.ShapeDtypeStruct(sens.shape, F32),
        ),
        in_specs=[any_place] * 2,
        out_specs=(any_place, any_place),
        scratch_shapes=[
            pltpu.VMEM(out.shape, F32), pltpu.VMEM(sens.shape, F32), dma((2, planes + 1)),
        ],
        compiler_params=pltpu.CompilerParams(vmem_limit_bytes=62 * 1024 * 1024),
    )(out, sens)
    return out.transpose(0, 2, 1, 3), sens


def solution(mesh):
    in_specs = (
        P("circ", "radax", None, None),
        P("circ", "radax", None, None),
        P(None, None, "circ", "radax", None, None),
        P(None, "circ", "radax", None, None),
        P(None, "circ", "radax", None, None),
        P(("circ", "radax")),
        P(("circ", "radax")),
        P(("circ", "radax"), None, None),
    )
    out_specs = (P("circ", "radax", None, None), P("circ", "radax"))
    return jax.shard_map(body, mesh=mesh, in_specs=in_specs, out_specs=out_specs, check_vma=False)
```

```python
import functools

import jax
import jax.numpy as jnp
from jax import lax
from jax.experimental import pallas as pl
from jax.experimental.pallas import tpu as pltpu
from jax.sharding import PartitionSpec as P

F32 = jnp.float32
BF16 = jnp.bfloat16
MESH = pl.DeviceIdType.MESH
FACE_ROWS = 128


def kernel(
    circs, rads,
    obj_hbm, adj_hbm, off_hbm, diag_hbm, pre_hbm, cell_ref, side_ref, dg_hbm,
    out_hbm, sens_ref,
    first, second, final, off, diag, pre, dg, rad_out, rad_in, picks, table, face_at, face_side,
    sens_out, sens_in,
    adj_sem, plane_sem, dg_sem, out_sem, circ_send, circ_recv, rad_send, rad_recv,
    rad2_send, rad2_recv, sens_send, sens_recv,
):
    planes, fields, rows, axial = obj_hbm.shape
    faces = cell_ref.shape[1]
    circ = lax.axis_index("circ")
    rad = lax.axis_index("radax")
    circ_up = lax.rem(circ + 1, circs)
    circ_down = lax.rem(circ + circs - 1, circs)

    def plane_loads(t):
        return [
            pltpu.make_async_copy(off_hbm.at[:, :, t], off.at[:, :, t], plane_sem.at[t, 0]),
            pltpu.make_async_copy(diag_hbm.at[:, t], diag.at[:, t], plane_sem.at[t, 1]),
            pltpu.make_async_copy(pre_hbm.at[:, t], pre.at[:, t], plane_sem.at[t, 2]),
            pltpu.make_async_copy(obj_hbm.at[t], final.at[t], plane_sem.at[t, 3]),
        ]

    adj_load = pltpu.make_async_copy(adj_hbm, first.at[pl.ds(1, planes)], adj_sem)
    dg_load = pltpu.make_async_copy(dg_hbm, dg, dg_sem)
    adj_load.start()
    order1 = [(p + planes - 3) % planes for p in range(planes)]
    for t in order1:
        for load in plane_loads(t):
            load.start()
    dg_load.start()

    barrier = pltpu.get_barrier_semaphore()
    others = [lax.rem(rad + d, rads) for d in range(1, rads)]
    for other in others:
        pl.semaphore_signal(barrier, inc=1, device_id=(circ, other), device_id_type=MESH)
    for side in (circ_up, circ_down):
        for other in [rad] + others:
            pl.semaphore_signal(barrier, inc=1, device_id=(side, other), device_id_type=MESH)
    pl.semaphore_wait(barrier, 3 * rads - 1)

    def circ_copy(application, upward):
        target = (second if application else first).at[0 if upward else planes + 1]
        if application:
            source = second.at[planes if upward else 1]
        else:
            source = adj_hbm.at[planes - 1 if upward else 0]
        return pltpu.make_async_remote_copy(
            src_ref=source, dst_ref=target,
            send_sem=circ_send.at[application, int(upward)],
            recv_sem=circ_recv.at[application, int(upward)],
            device_id=(circ_up if upward else circ_down, rad), device_id_type=MESH,
        )

    def rad_copy(upward):
        place = 0 if upward else 1
        return pltpu.make_async_remote_copy(
            src_ref=rad_out.at[0, place], dst_ref=rad_in.at[0, place],
            send_sem=rad_send.at[place], recv_sem=rad_recv.at[place],
            device_id=(circ, rad + 1 if upward else rad - 1), device_id_type=MESH,
        )

    def rad_plane_copy(upward, t):
        place = 0 if upward else 1
        return pltpu.make_async_remote_copy(
            src_ref=rad_out.at[1, place, t], dst_ref=rad_in.at[1, place, t],
            send_sem=rad2_send.at[place, t], recv_sem=rad2_recv.at[place, t],
            device_id=(circ, rad + 1 if upward else rad - 1), device_id_type=MESH,
        )

    has_lower = rad > 0
    has_upper = rad < rads - 1

    circ_copy(0, True).start()
    circ_copy(0, False).start()

    adj_load.wait()

    def edge_rows(t, carry):
        for j in range(fields):
            field = first[t + 1, j]
            rad_out[0, 0, t, j : j + 1, :] = field[rows - 1 : rows, :]
            rad_out[0, 1, t, j : j + 1, :] = field[0:1, :]
        return carry

    lax.fori_loop(0, planes, edge_rows, 0)

    @pl.when(has_upper)
    def _():
        rad_copy(True).start()

    @pl.when(has_lower)
    def _():
        rad_copy(False).start()

    @pl.when(rad == 0)
    def _():
        for application in range(2):
            rad_in[application, 0] = jnp.zeros(rad_in.shape[2:], F32)

    @pl.when(rad == rads - 1)
    def _():
        for application in range(2):
            rad_in[application, 1] = jnp.zeros(rad_in.shape[2:], F32)

    cells = cell_ref[...].astype(F32)
    row_of = jnp.floor((cells + 0.5) * (1.0 / axial))
    ax_of = cells - row_of * axial
    lanes = lax.broadcasted_iota(jnp.int32, (FACE_ROWS, planes * rows), 1).astype(F32)
    for f in range(0, faces, FACE_ROWS):
        def spread(values):
            part = values[:, f : f + FACE_ROWS]
            return jnp.transpose(jnp.broadcast_to(part, (FACE_ROWS, FACE_ROWS)))

        row_rep = spread(row_of)[:, 0:1]
        hot = jnp.where(lanes == row_rep, 1.0, 0.0).astype(BF16)
        picks[f : f + FACE_ROWS, 0 : planes * rows] = hot
        picks[f : f + FACE_ROWS, planes * rows : 2 * planes * rows] = hot
        face_at[f : f + FACE_ROWS, :] = spread(ax_of)
        face_side[f : f + FACE_ROWS, :] = spread(side_ref[...].astype(F32))

    row_index = lax.broadcasted_iota(jnp.int32, (rows, axial), 0)
    ax_index = lax.broadcasted_iota(jnp.int32, (rows, axial), 1)

    def apply_plane(source, application, t):
        def rad_lower(j):
            halo = rad_in[application, 0, t, j : j + 1, :]
            return jnp.where(row_index == 0, halo, pltpu.roll(source[t + 1, j], 1, 0))

        def rad_upper(j):
            halo = rad_in[application, 1, t, j : j + 1, :]
            return jnp.where(row_index == rows - 1, halo, pltpu.roll(source[t + 1, j], rows - 1, 0))

        def ax_lower(j):
            return jnp.where(ax_index == 0, 0.0, pltpu.roll(source[t + 1, j], 1, 1))

        def ax_upper(j):
            return jnp.where(ax_index == axial - 1, 0.0, pltpu.roll(source[t + 1, j], axial - 1, 1))

        beside = [
            lambda j: source[t, j],
            lambda j: source[t + 2, j],
            rad_lower, rad_upper, ax_lower, ax_upper,
        ]
        applied = [None] * fields
        for j in range(fields):
            vector = source[t + 1, j]
            for i in range(fields):
                term = diag[j, t, i].astype(F32) * vector
                applied[i] = term if j == 0 else applied[i] + term
        for k in range(6):
            for j in range(fields):
                vector = beside[k](j)
                for i in range(fields):
                    applied[i] = applied[i] + off[k, j, t, i].astype(F32) * vector
        residual = [final[t, i] - applied[i] for i in range(fields)]
        result = []
        for i in range(fields):
            value = pre[0, t, i].astype(F32) * residual[0]
            for j in range(1, fields):
                value = value + pre[j, t, i].astype(F32) * residual[j]
            result.append(source[t + 1, i] + value)
        return result

    @pl.when(has_lower)
    def _():
        rad_copy(True).wait_recv()

    @pl.when(has_upper)
    def _():
        rad_copy(False).wait_recv()

    def first_step(step, carry):
        t = lax.rem(step + (planes - 3), planes)

        @pl.when(step == 2)
        def _():
            circ_copy(0, True).wait_recv()
            circ_copy(0, False).wait_recv()

        for load in plane_loads(t):
            load.wait()
        result = apply_plane(first, 0, t)
        for i in range(fields):
            second[t + 1, i] = result[i]
            rad_out[1, 0, t, i : i + 1, :] = result[i][rows - 1 : rows, :]
            rad_out[1, 1, t, i : i + 1, :] = result[i][0:1, :]

        @pl.when(has_upper)
        def _():
            rad_plane_copy(True, t).start()

        @pl.when(has_lower)
        def _():
            rad_plane_copy(False, t).start()

        @pl.when(t == 0)
        def _():
            circ_copy(1, False).start()

        @pl.when(t == planes - 1)
        def _():
            circ_copy(1, True).start()

        return carry

    lax.fori_loop(0, planes, first_step, 0)

    def second_step(step, carry):
        t = lax.rem(step + 1, planes)

        @pl.when(step == planes - 2)
        def _():
            circ_copy(1, True).wait_recv()
            circ_copy(1, False).wait_recv()

        @pl.when(has_lower)
        def _():
            rad_plane_copy(True, t).wait_recv()

        @pl.when(has_upper)
        def _():
            rad_plane_copy(False, t).wait_recv()

        result = apply_plane(second, 1, t)
        for i in range(fields):
            high = result[i].astype(BF16)
            final[t, i] = result[i]
            table[i, t] = high
            table[i, t + planes] = (result[i] - high.astype(F32)).astype(BF16)
        pltpu.make_async_copy(final.at[t], out_hbm.at[t], out_sem.at[t]).start()
        return carry

    lax.fori_loop(0, planes, second_step, 0)

    dg_load.wait()
    place = lax.broadcasted_iota(jnp.int32, (FACE_ROWS, axial), 1).astype(F32)

    def face_step(step, carry):
        lower, upper = carry
        part = pl.ds(pl.multiple_of(step * FACE_ROWS, FACE_ROWS), FACE_ROWS)
        hot = picks[part, :]
        at = face_at[part, :][:, 0:1]
        side = face_side[part, :]
        total = None
        for i in range(fields):
            values = table[i].reshape(2 * planes * rows, axial)
            row = jnp.dot(hot, values, preferred_element_type=F32)
            picked = jnp.sum(jnp.where(place == at, row, 0.0), axis=1, keepdims=True)
            term = picked * dg[i, part, :]
            total = term if i == 0 else total + term
        lower = lower + jnp.sum(jnp.where(side == 0.0, total, 0.0), axis=0, keepdims=True)
        upper = upper + jnp.sum(jnp.where(side == 1.0, total, 0.0), axis=0, keepdims=True)
        return lower, upper

    zero = jnp.zeros((1, dg.shape[2]), F32)
    lower, upper = lax.fori_loop(0, faces // FACE_ROWS, face_step, (zero, zero))
    sens_out[0] = jnp.broadcast_to(lower, sens_out.shape[1:])
    sens_out[1] = jnp.broadcast_to(upper, sens_out.shape[1:])

    def sens_copy(side, d):
        return pltpu.make_async_remote_copy(
            src_ref=sens_out.at[side], dst_ref=sens_in.at[side, d],
            send_sem=sens_send.at[side, d], recv_sem=sens_recv.at[side, d],
            device_id=(circ_up if side else circ, lax.rem(rad + d, rads)), device_id_type=MESH,
        )

    sends = [(1, d) for d in range(rads)] + [(0, d) for d in range(1, rads)]
    for side, d in sends:
        sens_copy(side, d).start()
    total = lower
    for side, d in sends:
        sens_copy(side, d).wait_recv()
        total = total + sens_in[side, d, 0:1, :]
    owned = sens_ref.shape[1]
    mine = total[:, 0:owned]
    for block in range(1, rads):
        mine = jnp.where(rad == block, total[:, block * owned : (block + 1) * owned], mine)
    sens_ref[...] = mine

    for side, d in sends:
        sens_copy(side, d).wait_send()
    for application in range(2):
        for upward in (True, False):
            circ_copy(application, upward).wait_send()

    @pl.when(has_upper)
    def _():
        rad_copy(True).wait_send()
        for t in range(planes):
            rad_plane_copy(True, t).wait_send()

    @pl.when(has_lower)
    def _():
        rad_copy(False).wait_send()
        for t in range(planes):
            rad_plane_copy(False, t).wait_send()

    for t in range(planes):
        pltpu.make_async_copy(final.at[t], out_hbm.at[t], out_sem.at[t]).wait()


def hand_over(state_ref, sens_ref, state_out, sens_out, state, sens, sems):
    planes = state.shape[0]
    places = [(state_ref.at[t], state.at[t], state_out.at[t]) for t in range(planes)]
    places.append((sens_ref, sens, sens_out))
    into = [pltpu.make_async_copy(a, b, sems.at[0, n]) for n, (a, b, c) in enumerate(places)]
    onto = [pltpu.make_async_copy(b, c, sems.at[1, n]) for n, (a, b, c) in enumerate(places)]
    for copy in into:
        copy.start()
    for n, copy in enumerate(into):
        copy.wait()
        onto[n].start()
    for copy in onto:
        copy.wait()


def body(
    objective_grad, adjoint_start, jac_off, jac_diag, precond, face_cell, face_side, design_grad
):
    circs, rads = lax.axis_size("circ"), lax.axis_size("radax")
    planes, rows, fields, axial = adjoint_start.shape
    faces, _, variables = design_grad.shape
    state = (planes, fields, rows, axial)
    any_place = pl.BlockSpec(memory_space=pl.ANY)
    in_vmem = pl.BlockSpec(memory_space=pltpu.VMEM)
    dma = pltpu.SemaphoreType.DMA
    out, sens = pl.pallas_call(
        functools.partial(kernel, circs, rads),
        out_shape=(
            jax.ShapeDtypeStruct(state, F32),
            jax.ShapeDtypeStruct((1, variables // rads), F32),
        ),
        in_specs=[any_place] * 5 + [in_vmem] * 2 + [any_place],
        out_specs=(any_place, in_vmem),
        scratch_shapes=[
            pltpu.VMEM((planes + 2, fields, rows, axial), F32),
            pltpu.VMEM((planes + 2, fields, rows, axial), F32),
            pltpu.VMEM(state, F32),
            pltpu.VMEM((6, fields) + state, BF16),
            pltpu.VMEM((fields,) + state, BF16),
            pltpu.VMEM((fields,) + state, BF16),
            pltpu.VMEM((fields, faces, variables), F32),
            pltpu.VMEM((2, 2, planes, fields, axial), F32),
            pltpu.VMEM((2, 2, planes, fields, axial), F32),
            pltpu.VMEM((faces, 2 * planes * rows), BF16),
            pltpu.VMEM((fields, 2 * planes, rows, axial), BF16),
            pltpu.VMEM((faces, FACE_ROWS), F32),
            pltpu.VMEM((faces, FACE_ROWS), F32),
            pltpu.VMEM((2, 8, variables), F32),
            pltpu.VMEM((2, rads, 8, variables), F32),
            dma, dma((planes, 4)), dma, dma((planes,)),
            dma((2, 2)), dma((2, 2)), dma((2,)), dma((2,)),
            dma((2, planes)), dma((2, planes)), dma((2, rads)), dma((2, rads)),
        ],
        compiler_params=pltpu.CompilerParams(
            collective_id=0, has_side_effects=True, vmem_limit_bytes=62 * 1024 * 1024
        ),
        cost_estimate=pl.CostEstimate(
            flops=4 * 48 * fields * planes * rows * axial,
            bytes_accessed=48 * 2 * fields * planes * rows * axial,
            transcendentals=0,
        ),
    )(
        objective_grad.transpose(0, 2, 1, 3),
        adjoint_start.transpose(0, 2, 1, 3),
        jac_off.transpose(0, 1, 2, 4, 3, 5),
        jac_diag.transpose(0, 1, 3, 2, 4),
        precond.transpose(0, 1, 3, 2, 4),
        face_cell.reshape(1, faces),
        face_side.reshape(1, faces),
        design_grad.transpose(1, 0, 2),
    )
    out, sens = pl.pallas_call(
        hand_over,
        out_shape=(
            jax.ShapeDtypeStruct(out.shape, F32),
            jax.ShapeDtypeStruct(sens.shape, F32),
        ),
        in_specs=[any_place] * 2,
        out_specs=(any_place, any_place),
        scratch_shapes=[
            pltpu.VMEM(out.shape, F32), pltpu.VMEM(sens.shape, F32), dma((2, planes + 1)),
        ],
        compiler_params=pltpu.CompilerParams(vmem_limit_bytes=62 * 1024 * 1024),
    )(out, sens)
    return out.transpose(0, 2, 1, 3), sens


def solution(mesh):
    in_specs = (
        P("circ", "radax", None, None),
        P("circ", "radax", None, None),
        P(None, None, "circ", "radax", None, None),
        P(None, "circ", "radax", None, None),
        P(None, "circ", "radax", None, None),
        P(("circ", "radax")),
        P(("circ", "radax")),
        P(("circ", "radax"), None, None),
    )
    out_specs = (P("circ", "radax", None, None), P("circ", "radax"))
    return jax.shard_map(body, mesh=mesh, in_specs=in_specs, out_specs=out_specs, check_vma=False)
```

```python
import functools

import jax
import jax.numpy as jnp
from jax import lax
from jax.experimental import pallas as pl
from jax.experimental.pallas import tpu as pltpu
from jax.sharding import PartitionSpec as P

F32 = jnp.float32
BF16 = jnp.bfloat16
MESH = pl.DeviceIdType.MESH
FACE_ROWS = 128


def kernel(
    circs, rads,
    obj_hbm, adj_hbm, off_hbm, diag_hbm, pre_hbm, cell_ref, side_ref, dg_hbm,
    out_hbm, sens_ref,
    states, final, off, diag, pre, dg, rad_out, rad_in, picks, table, face_at, face_side, latest,
    sens_out, sens_in,
    adj_sem, plane_sem, dg_sem, out_sem, circ_send, circ_recv, rad_send, rad_recv,
    rad2_send, rad2_recv, sens_send, sens_recv,
):
    planes, fields, rows, axial = obj_hbm.shape
    faces = cell_ref.shape[1]
    circ = lax.axis_index("circ")
    rad = lax.axis_index("radax")
    circ_up = lax.rem(circ + 1, circs)
    circ_down = lax.rem(circ + circs - 1, circs)

    def plane_loads(t):
        return [
            pltpu.make_async_copy(off_hbm.at[:, :, t], off.at[:, :, t], plane_sem.at[t, 0]),
            pltpu.make_async_copy(diag_hbm.at[:, t], diag.at[:, t], plane_sem.at[t, 1]),
            pltpu.make_async_copy(pre_hbm.at[:, t], pre.at[:, t], plane_sem.at[t, 2]),
            pltpu.make_async_copy(obj_hbm.at[t], final.at[t], plane_sem.at[t, 3]),
        ]

    adj_load = pltpu.make_async_copy(adj_hbm, states.at[0, pl.ds(1, planes)], adj_sem)
    dg_load = pltpu.make_async_copy(dg_hbm, dg, dg_sem)
    adj_load.start()
    order1 = [(p + planes - 3) % planes for p in range(planes)]
    for t in order1:
        for load in plane_loads(t):
            load.start()
    dg_load.start()

    barrier = pltpu.get_barrier_semaphore()
    others = [lax.rem(rad + d, rads) for d in range(1, rads)]
    for other in others:
        pl.semaphore_signal(barrier, inc=1, device_id=(circ, other), device_id_type=MESH)
    for side in (circ_up, circ_down):
        for other in [rad] + others:
            pl.semaphore_signal(barrier, inc=1, device_id=(side, other), device_id_type=MESH)
    pl.semaphore_wait(barrier, 3 * rads - 1)

    def circ_copy(application, upward):
        target = states.at[application, 0 if upward else planes + 1]
        if application:
            source = states.at[1, planes if upward else 1]
        else:
            source = adj_hbm.at[planes - 1 if upward else 0]
        return pltpu.make_async_remote_copy(
            src_ref=source, dst_ref=target,
            send_sem=circ_send.at[application, int(upward)],
            recv_sem=circ_recv.at[application, int(upward)],
            device_id=(circ_up if upward else circ_down, rad), device_id_type=MESH,
        )

    def rad_copy(upward):
        place = 0 if upward else 1
        return pltpu.make_async_remote_copy(
            src_ref=rad_out.at[0, place], dst_ref=rad_in.at[0, place],
            send_sem=rad_send.at[place], recv_sem=rad_recv.at[place],
            device_id=(circ, rad + 1 if upward else rad - 1), device_id_type=MESH,
        )

    def rad_plane_copy(upward, t):
        place = 0 if upward else 1
        return pltpu.make_async_remote_copy(
            src_ref=rad_out.at[1, place, t], dst_ref=rad_in.at[1, place, t],
            send_sem=rad2_send.at[place, t], recv_sem=rad2_recv.at[place, t],
            device_id=(circ, rad + 1 if upward else rad - 1), device_id_type=MESH,
        )

    has_lower = rad > 0
    has_upper = rad < rads - 1

    circ_copy(0, True).start()
    circ_copy(0, False).start()

    adj_load.wait()

    def edge_rows(t, carry):
        for j in range(fields):
            field = states[0, t + 1, j]
            rad_out[0, 0, t, j : j + 1, :] = field[rows - 1 : rows, :]
            rad_out[0, 1, t, j : j + 1, :] = field[0:1, :]
        return carry

    lax.fori_loop(0, planes, edge_rows, 0)

    @pl.when(has_upper)
    def _():
        rad_copy(True).start()

    @pl.when(has_lower)
    def _():
        rad_copy(False).start()

    @pl.when(rad == 0)
    def _():
        for application in range(2):
            rad_in[application, 0] = jnp.zeros(rad_in.shape[2:], F32)

    @pl.when(rad == rads - 1)
    def _():
        for application in range(2):
            rad_in[application, 1] = jnp.zeros(rad_in.shape[2:], F32)

    cells = cell_ref[...].astype(F32)
    row_of = jnp.floor((cells + 0.5) * (1.0 / axial))
    ax_of = cells - row_of * axial
    lanes = lax.broadcasted_iota(jnp.int32, (FACE_ROWS, planes * rows), 1).astype(F32)
    for f in range(0, faces, FACE_ROWS):
        def spread(values):
            part = values[:, f : f + FACE_ROWS]
            return jnp.transpose(jnp.broadcast_to(part, (FACE_ROWS, FACE_ROWS)))

        row_rep = spread(row_of)[:, 0:1]
        hot = jnp.where(lanes == row_rep, 1.0, 0.0).astype(BF16)
        picks[f : f + FACE_ROWS, 0 : planes * rows] = hot
        picks[f : f + FACE_ROWS, planes * rows : 2 * planes * rows] = hot
        face_at[f : f + FACE_ROWS, :] = spread(ax_of)
        face_side[f : f + FACE_ROWS, :] = spread(side_ref[...].astype(F32))

    row_index = lax.broadcasted_iota(jnp.int32, (rows, axial), 0)
    ax_index = lax.broadcasted_iota(jnp.int32, (rows, axial), 1)

    def apply_plane(application, t):
        def rad_lower(j):
            halo = rad_in[application, 0, t, j : j + 1, :]
            return jnp.where(row_index == 0, halo, pltpu.roll(states[application, t + 1, j], 1, 0))

        def rad_upper(j):
            halo = rad_in[application, 1, t, j : j + 1, :]
            return jnp.where(row_index == rows - 1, halo, pltpu.roll(states[application, t + 1, j], rows - 1, 0))

        def ax_lower(j):
            return jnp.where(ax_index == 0, 0.0, pltpu.roll(states[application, t + 1, j], 1, 1))

        def ax_upper(j):
            return jnp.where(ax_index == axial - 1, 0.0, pltpu.roll(states[application, t + 1, j], axial - 1, 1))

        beside = [
            lambda j: states[application, t, j],
            lambda j: states[application, t + 2, j],
            rad_lower, rad_upper, ax_lower, ax_upper,
        ]
        applied = [None] * fields
        for j in range(fields):
            vector = states[application, t + 1, j]
            for i in range(fields):
                term = diag[j, t, i].astype(F32) * vector
                applied[i] = term if j == 0 else applied[i] + term
        for k in range(6):
            for j in range(fields):
                vector = beside[k](j)
                for i in range(fields):
                    applied[i] = applied[i] + off[k, j, t, i].astype(F32) * vector
        residual = [final[t, i] - applied[i] for i in range(fields)]
        result = []
        for i in range(fields):
            value = pre[0, t, i].astype(F32) * residual[0]
            for j in range(1, fields):
                value = value + pre[j, t, i].astype(F32) * residual[j]
            result.append(states[application, t + 1, i] + value)
        return result

    @pl.when(has_lower)
    def _():
        rad_copy(True).wait_recv()

    @pl.when(has_upper)
    def _():
        rad_copy(False).wait_recv()

    def plane_step(step, carry):
        application = step // planes
        t = lax.rem(step + (planes - 3) + 4 * application, planes)

        for before, place in ((0, 2), (1, 2 * planes - 2)):
            @pl.when(step == place)
            def _():
                circ_copy(before, True).wait_recv()
                circ_copy(before, False).wait_recv()

        @pl.when(application == 0)
        def _():
            for load in plane_loads(t):
                load.wait()

        @pl.when(application == 1)
        def _():
            @pl.when(has_lower)
            def _():
                rad_plane_copy(True, t).wait_recv()

            @pl.when(has_upper)
            def _():
                rad_plane_copy(False, t).wait_recv()

        result = apply_plane(application, t)
        for i in range(fields):
            latest[i] = result[i]

        @pl.when(application == 0)
        def _():
            for i in range(fields):
                value = latest[i]
                states[1, t + 1, i] = value
                rad_out[1, 0, t, i : i + 1, :] = value[rows - 1 : rows, :]
                rad_out[1, 1, t, i : i + 1, :] = value[0:1, :]

            @pl.when(has_upper)
            def _():
                rad_plane_copy(True, t).start()

            @pl.when(has_lower)
            def _():
                rad_plane_copy(False, t).start()

            @pl.when(t == 0)
            def _():
                circ_copy(1, False).start()

            @pl.when(t == planes - 1)
            def _():
                circ_copy(1, True).start()

        @pl.when(application == 1)
        def _():
            for i in range(fields):
                value = latest[i]
                high = value.astype(BF16)
                final[t, i] = value
                table[i, t] = high
                table[i, t + planes] = (value - high.astype(F32)).astype(BF16)
            pltpu.make_async_copy(final.at[t], out_hbm.at[t], out_sem.at[t]).start()

        return carry

    lax.fori_loop(0, 2 * planes, plane_step, 0)

    dg_load.wait()
    place = lax.broadcasted_iota(jnp.int32, (FACE_ROWS, axial), 1).astype(F32)

    def face_step(step, carry):
        lower, upper = carry
        part = pl.ds(pl.multiple_of(step * FACE_ROWS, FACE_ROWS), FACE_ROWS)
        hot = picks[part, :]
        at = face_at[part, :][:, 0:1]
        side = face_side[part, :]
        total = None
        for i in range(fields):
            values = table[i].reshape(2 * planes * rows, axial)
            row = jnp.dot(hot, values, preferred_element_type=F32)
            picked = jnp.sum(jnp.where(place == at, row, 0.0), axis=1, keepdims=True)
            term = picked * dg[i, part, :]
            total = term if i == 0 else total + term
        lower = lower + jnp.sum(jnp.where(side == 0.0, total, 0.0), axis=0, keepdims=True)
        upper = upper + jnp.sum(jnp.where(side == 1.0, total, 0.0), axis=0, keepdims=True)
        return lower, upper

    zero = jnp.zeros((1, dg.shape[2]), F32)
    lower, upper = lax.fori_loop(0, faces // FACE_ROWS, face_step, (zero, zero))
    sens_out[0] = jnp.broadcast_to(lower, sens_out.shape[1:])
    sens_out[1] = jnp.broadcast_to(upper, sens_out.shape[1:])

    def sens_copy(side, d):
        return pltpu.make_async_remote_copy(
            src_ref=sens_out.at[side], dst_ref=sens_in.at[side, d],
            send_sem=sens_send.at[side, d], recv_sem=sens_recv.at[side, d],
            device_id=(circ_up if side else circ, lax.rem(rad + d, rads)), device_id_type=MESH,
        )

    sends = [(1, d) for d in range(rads)] + [(0, d) for d in range(1, rads)]
    for side, d in sends:
        sens_copy(side, d).start()
    total = lower
    for side, d in sends:
        sens_copy(side, d).wait_recv()
        total = total + sens_in[side, d, 0:1, :]
    owned = sens_ref.shape[1]
    mine = total[:, 0:owned]
    for block in range(1, rads):
        mine = jnp.where(rad == block, total[:, block * owned : (block + 1) * owned], mine)
    sens_ref[...] = mine

    for side, d in sends:
        sens_copy(side, d).wait_send()
    for application in range(2):
        for upward in (True, False):
            circ_copy(application, upward).wait_send()

    @pl.when(has_upper)
    def _():
        rad_copy(True).wait_send()
        for t in range(planes):
            rad_plane_copy(True, t).wait_send()

    @pl.when(has_lower)
    def _():
        rad_copy(False).wait_send()
        for t in range(planes):
            rad_plane_copy(False, t).wait_send()

    for t in range(planes):
        pltpu.make_async_copy(final.at[t], out_hbm.at[t], out_sem.at[t]).wait()


def hand_over(state_ref, sens_ref, state_out, sens_out, state, sens, sems):
    planes = state.shape[0]
    places = [(state_ref.at[t], state.at[t], state_out.at[t]) for t in range(planes)]
    places.append((sens_ref, sens, sens_out))
    into = [pltpu.make_async_copy(a, b, sems.at[0, n]) for n, (a, b, c) in enumerate(places)]
    onto = [pltpu.make_async_copy(b, c, sems.at[1, n]) for n, (a, b, c) in enumerate(places)]
    for copy in into:
        copy.start()
    for n, copy in enumerate(into):
        copy.wait()
        onto[n].start()
    for copy in onto:
        copy.wait()


def body(
    objective_grad, adjoint_start, jac_off, jac_diag, precond, face_cell, face_side, design_grad
):
    circs, rads = lax.axis_size("circ"), lax.axis_size("radax")
    planes, rows, fields, axial = adjoint_start.shape
    faces, _, variables = design_grad.shape
    state = (planes, fields, rows, axial)
    any_place = pl.BlockSpec(memory_space=pl.ANY)
    in_vmem = pl.BlockSpec(memory_space=pltpu.VMEM)
    dma = pltpu.SemaphoreType.DMA
    out, sens = pl.pallas_call(
        functools.partial(kernel, circs, rads),
        out_shape=(
            jax.ShapeDtypeStruct(state, F32),
            jax.ShapeDtypeStruct((1, variables // rads), F32),
        ),
        in_specs=[any_place] * 5 + [in_vmem] * 2 + [any_place],
        out_specs=(any_place, in_vmem),
        scratch_shapes=[
            pltpu.VMEM((2, planes + 2, fields, rows, axial), F32),
            pltpu.VMEM(state, F32),
            pltpu.VMEM((6, fields) + state, BF16),
            pltpu.VMEM((fields,) + state, BF16),
            pltpu.VMEM((fields,) + state, BF16),
            pltpu.VMEM((fields, faces, variables), F32),
            pltpu.VMEM((2, 2, planes, fields, axial), F32),
            pltpu.VMEM((2, 2, planes, fields, axial), F32),
            pltpu.VMEM((faces, 2 * planes * rows), BF16),
            pltpu.VMEM((fields, 2 * planes, rows, axial), BF16),
            pltpu.VMEM((faces, FACE_ROWS), F32),
            pltpu.VMEM((faces, FACE_ROWS), F32),
            pltpu.VMEM((fields, rows, axial), F32),
            pltpu.VMEM((2, 8, variables), F32),
            pltpu.VMEM((2, rads, 8, variables), F32),
            dma, dma((planes, 4)), dma, dma((planes,)),
            dma((2, 2)), dma((2, 2)), dma((2,)), dma((2,)),
            dma((2, planes)), dma((2, planes)), dma((2, rads)), dma((2, rads)),
        ],
        compiler_params=pltpu.CompilerParams(
            collective_id=0, has_side_effects=True, vmem_limit_bytes=62 * 1024 * 1024
        ),
        cost_estimate=pl.CostEstimate(
            flops=4 * 48 * fields * planes * rows * axial,
            bytes_accessed=48 * 2 * fields * planes * rows * axial,
            transcendentals=0,
        ),
    )(
        objective_grad.transpose(0, 2, 1, 3),
        adjoint_start.transpose(0, 2, 1, 3),
        jac_off.transpose(0, 1, 2, 4, 3, 5),
        jac_diag.transpose(0, 1, 3, 2, 4),
        precond.transpose(0, 1, 3, 2, 4),
        face_cell.reshape(1, faces),
        face_side.reshape(1, faces),
        design_grad.transpose(1, 0, 2),
    )
    out, sens = pl.pallas_call(
        hand_over,
        out_shape=(
            jax.ShapeDtypeStruct(out.shape, F32),
            jax.ShapeDtypeStruct(sens.shape, F32),
        ),
        in_specs=[any_place] * 2,
        out_specs=(any_place, any_place),
        scratch_shapes=[
            pltpu.VMEM(out.shape, F32), pltpu.VMEM(sens.shape, F32), dma((2, planes + 1)),
        ],
        compiler_params=pltpu.CompilerParams(vmem_limit_bytes=62 * 1024 * 1024),
    )(out, sens)
    return out.transpose(0, 2, 1, 3), sens


def solution(mesh):
    in_specs = (
        P("circ", "radax", None, None),
        P("circ", "radax", None, None),
        P(None, None, "circ", "radax", None, None),
        P(None, "circ", "radax", None, None),
        P(None, "circ", "radax", None, None),
        P(("circ", "radax")),
        P(("circ", "radax")),
        P(("circ", "radax"), None, None),
    )
    out_specs = (P("circ", "radax", None, None), P("circ", "radax"))
    return jax.shard_map(body, mesh=mesh, in_specs=in_specs, out_specs=out_specs, check_vma=False)
```
